32 devices in a mesh: rep: 4 (over y, x), blk: 8 (over z, core).
Axes of the slice: x: 2, y: 2, z: 4, core: 2. Of those that a mesh axis runs over, the one named last changes fastest.
Arguments:
- features: bfloat16 [8, 2048, 128], P('blk', 'rep'), may hold values from -6 to 6
- weight: bfloat16 [128, 256], replicated, may hold values from -0.5 to 0.5
- cotangent: bfloat16 [8, 2048, 256], P('blk', 'rep'), may hold values from -6 to 6
- self_weight: float32 [8, 2048], P('blk', 'rep'), may hold values from 0.3 to 1.5
- block_rows: int32 [4, 8, 384], P('rep', 'blk'), may hold values from 0 to 31, as said below
- block_cols: int32 [4, 8, 384], P('rep', 'blk'), may hold values from 0 to 15, as said below
- block_counts: int32 [4, 8], P('rep', 'blk'), may hold values from 1 to 384, as said below
- block_values: bfloat16 [4, 8, 384, 128, 128], P('rep', 'blk'), as said below
Outputs:
- activated: bfloat16 [8, 2048, 256], P('blk', 'rep')
- feature_grad: bfloat16 [8, 2048, 128], P('blk', 'rep')
- weight_grad: float32 [128, 256], P('rep')
The draws below stay inside these ranges and needn't reach their ends.
Inputs may be any that keep to these rules, and one draw needn't show every extreme that they name: `block_counts`: one device of every draw has all 384 slots live. `block_rows`: the live slots of one device name distinct (row tile, column tile) pairs; slots past the count hold 0. `block_cols`: slots past the count hold 0. `block_values`: slots at or past a device's count hold zeros.
All inputs are finite; a program needn't handle non-finite values.
Results may differ from the reference program's by a relative error of at most 0.024.
Values may be sent and summed in bfloat16 or wider, within the bound.
A program may use at most 128 MiB of HBM per device.

```python
import math
import jax
import jax.numpy as jnp
from jax import lax

F = 128
H = 256
BS = 128
ROWS_DEV = 512
CAP = 384
PANEL_ROWS = 2048
N_REP = 4
N_BLK = 8


def block_layout(key):
    row_tiles = N_BLK * ROWS_DEV // BS
    col_tiles = N_REP * ROWS_DEV // BS
    device_total = N_REP * N_BLK
    spread = jax.random.randint(jax.random.fold_in(key, 11), (device_total,), CAP // 6, CAP // 2 + 1)
    busiest = jax.random.randint(jax.random.fold_in(key, 12), (), 0, device_total)
    count_list = jnp.where(jnp.arange(device_total) == busiest, CAP, spread).astype(jnp.int32)
    key_list = jax.random.split(jax.random.fold_in(key, 13), device_total)
    pair_ids = jax.vmap(lambda one_key: jax.random.permutation(one_key, row_tiles * col_tiles)[:CAP])(key_list)
    is_live = jnp.arange(CAP)[None, :] < count_list[:, None]
    tile_rows = jnp.where(is_live, pair_ids // col_tiles, 0).astype(jnp.int32)
    tile_cols = jnp.where(is_live, pair_ids % col_tiles, 0).astype(jnp.int32)
    return (count_list, tile_rows, tile_cols)


def draw_block_counts(key, part):
    shared = block_layout(key)
    return shared[0].reshape(N_REP, N_BLK)


def draw_block_rows(key, part):
    shared = block_layout(key)
    return shared[1].reshape(N_REP, N_BLK, CAP)


def draw_block_cols(key, part):
    shared = block_layout(key)
    return shared[2].reshape(N_REP, N_BLK, CAP)


def draw_block_values(key, part):
    shared = block_layout(key)
    key = jax.random.fold_in(key, 4)
    scale = (6.0 * ROWS_DEV / (CAP * BS * BS)) ** 0.5
    live_rows = (jnp.arange(CAP)[None, :] < shared[0][:, None]).astype(jnp.float32)

    def one_device(inputs):
        index, live_row = inputs
        dev_key = jax.random.fold_in(key, index)
        keep = jax.random.bernoulli(jax.random.fold_in(dev_key, 1), 0.5, (CAP, BS, BS)).astype(jnp.float32)
        entries = jax.random.normal(jax.random.fold_in(dev_key, 2), (CAP, BS, BS), jnp.float32)
        return (entries * keep * scale * live_row[:, None, None]).astype(jnp.bfloat16)
    tiles_all = lax.map(one_device, (jnp.arange(N_REP * N_BLK, dtype=jnp.int32), live_rows))
    return tiles_all.reshape(N_REP, N_BLK, CAP, BS, BS)


def block_levels(key, dims, shards, least, top_value):
    factor_of = 1.0
    for axis_at, parts in shards:
        heights = jax.random.uniform(jax.random.fold_in(jax.random.fold_in(key, 6), axis_at), (parts,), jnp.float32, least / len(shards), top_value / len(shards))
        factor_of = factor_of * jnp.repeat(jnp.exp(heights), dims[axis_at] // parts).reshape((-1,) + (1,) * (len(dims) - 1 - axis_at))
    return factor_of


def scatter_about(key, shape, width, limit, pieces=(), held_as=jnp.bfloat16):
    gain = block_levels(key, shape, pieces, -0.22, 0.18) if pieces else 1.0
    array = jax.random.normal(key, shape, jnp.float32) * width * gain
    return jnp.minimum(jnp.maximum(array, -limit), limit).astype(held_as)


def setup_inputs(seed: int = 0) -> dict:
    key_of = jax.random.split(jax.random.key(seed), 9)
    return {
        "features": scatter_about(key_of[0], (N_BLK, PANEL_ROWS, F), 1.0, 6.0, ((0, 8), (1, 4))),
        "weight": scatter_about(key_of[1], (F, H), F ** -0.5, 0.5),
        "cotangent": scatter_about(key_of[2], (N_BLK, PANEL_ROWS, H), 1.0, 6.0, ((0, 8), (1, 4))),
        "self_weight": jnp.clip(jnp.exp(math.log(1.5) - 1.60943787 * jax.random.uniform(key_of[3], (N_BLK, PANEL_ROWS), jnp.float32) ** block_levels(key_of[3], (N_BLK, PANEL_ROWS), ((0, 8), (1, 4)), -0.2, 0.2)), 0.3, 1.5),
        "block_rows": draw_block_rows(jax.random.fold_in(key_of[8], 71), 0),
        "block_cols": draw_block_cols(jax.random.fold_in(key_of[8], 71), 0),
        "block_counts": draw_block_counts(jax.random.fold_in(key_of[8], 71), 0),
        "block_values": draw_block_values(jax.random.fold_in(key_of[8], 71), 0),
    }


def silu_slope(pre_act):
    sigma = jax.nn.sigmoid(pre_act)
    return sigma * (1.0 + pre_act * (1.0 - sigma))

def reference(features, weight, cotangent, self_weight, block_rows, block_cols, block_counts, block_values):
    panel_rows = N_REP * ROWS_DEV
    row_tiles = N_BLK * ROWS_DEV // BS
    col_tiles = panel_rows // BS
    slot_ids = jnp.arange(CAP, dtype=jnp.int32)
    device_ids = jnp.arange(N_REP * N_BLK, dtype=jnp.int32)

    def device_tiles(index):
        rep_at = index // N_BLK
        blk_at = index % N_BLK
        tile_data = block_values[rep_at, blk_at].astype(jnp.float32)
        is_live = (slot_ids < block_counts[rep_at, blk_at]).astype(jnp.float32)
        return (rep_at, blk_at, tile_data * is_live[:, None, None], block_rows[rep_at, blk_at], block_cols[rep_at, blk_at])

    def forward_step(summed, index):
        rep_at, blk_at, tile_data, rows_here, cols_here = device_tiles(index)
        panel = lax.dynamic_index_in_dim(features, blk_at, 0, keepdims=False).astype(jnp.float32)
        panel = panel.reshape(col_tiles, BS, F)
        products = jnp.einsum('sij,sjf->sif', tile_data, panel[cols_here])
        term = jnp.zeros((row_tiles, BS, F), jnp.float32).at[rows_here].add(products)
        term = lax.optimization_barrier(term.astype(jnp.bfloat16)).astype(jnp.float32)
        term = term.reshape(N_BLK, 1, ROWS_DEV, F)
        current = lax.dynamic_slice_in_dim(summed, rep_at, 1, 1)
        return (lax.dynamic_update_slice_in_dim(summed, current + term, rep_at, 1), None)
    summed = lax.scan(forward_step, jnp.zeros((N_BLK, N_REP, ROWS_DEV, F), jnp.float32), device_ids)[0]
    own_rows = features.astype(jnp.float32)
    aggregated = (summed.reshape(N_BLK, panel_rows, F) + self_weight[:, :, None] * own_rows).astype(jnp.bfloat16)
    flat_agg = aggregated.reshape(N_BLK * panel_rows, F)
    pre_act = jnp.dot(flat_agg, weight, preferred_element_type=jnp.float32)
    activated = jax.nn.silu(pre_act).astype(jnp.bfloat16)
    slope = (cotangent.reshape(N_BLK * panel_rows, H).astype(jnp.float32) * silu_slope(pre_act)).astype(jnp.bfloat16)
    weight_grad = jnp.dot(flat_agg.T, slope, preferred_element_type=jnp.float32) / math.sqrt(N_BLK * panel_rows)
    row_grad = jnp.dot(slope, weight.T, preferred_element_type=jnp.float32).astype(jnp.bfloat16)
    grid_grad = row_grad.reshape(N_BLK, N_REP, ROWS_DEV, F)

    def backward_step(columns, index):
        rep_at, blk_at, tile_data, rows_here, cols_here = device_tiles(index)
        source = lax.dynamic_index_in_dim(grid_grad, rep_at, 1, keepdims=False).astype(jnp.float32)
        source = source.reshape(row_tiles, BS, F)
        products = jnp.einsum('sji,sjf->sif', tile_data, source[rows_here])
        term = jnp.zeros((col_tiles, BS, F), jnp.float32).at[cols_here].add(products)
        term = term.reshape(1, panel_rows, F)
        current = lax.dynamic_slice_in_dim(columns, blk_at, 1, 0)
        return (lax.dynamic_update_slice_in_dim(columns, current + term, blk_at, 0), None)
    columns = lax.scan(backward_step, jnp.zeros((N_BLK, panel_rows, F), jnp.float32), device_ids)[0]
    own_grad = self_weight[:, :, None] * row_grad.reshape(N_BLK, panel_rows, F).astype(jnp.float32)
    feature_grad = (columns + own_grad).astype(jnp.bfloat16)
    return (activated.reshape(N_BLK, panel_rows, H), feature_grad, weight_grad)
```

```python
import functools
import math

import jax
import jax.numpy as jnp
from jax import lax
from jax.experimental import pallas as pl
from jax.experimental.pallas import tpu as pltpu
from jax.sharding import PartitionSpec as P

group_slots = 32


def silu_slope(pre_act):
    sigma = jax.nn.sigmoid(pre_act)
    return sigma * (1.0 + pre_act * (1.0 - sigma))


def tile_products(tile_values, row_index, col_index, live_count, source, targets, flipped):
    feat_width = source.shape[-1]
    tile_side = tile_values.shape[-1]
    start_sums = jnp.zeros((targets, tile_side, feat_width), jnp.float32)
    turn_count = (live_count + group_slots - 1) // group_slots

    def one_group(step_index, summed):
        first_slot = step_index * group_slots
        tile_block = lax.dynamic_slice_in_dim(tile_values, first_slot, group_slots, 0)
        rows_here = lax.dynamic_slice_in_dim(row_index, first_slot, group_slots, 0)
        cols_here = lax.dynamic_slice_in_dim(col_index, first_slot, group_slots, 0)
        is_live = (first_slot + jnp.arange(group_slots, dtype=jnp.int32) < live_count).astype(
            jnp.float32
        )
        if flipped:
            picked = source[rows_here]
            products = jnp.einsum(
                "gji,gjf->gif", tile_block, picked, preferred_element_type=jnp.float32
            )
            landing = cols_here
        else:
            picked = source[cols_here]
            products = jnp.einsum(
                "gij,gjf->gif", tile_block, picked, preferred_element_type=jnp.float32
            )
            landing = rows_here
        return summed.at[landing].add(products * is_live[:, None, None])

    return lax.fori_loop(0, turn_count, one_group, start_sums)


cores = 2
load_parts = 8
dense_limit = 20 * 2**20
vmem_bytes = 52 * 2**20
MESH = pl.DeviceIdType.MESH


def flip(place, mask):
    bit = 1
    while bit <= mask:
        if mask & bit:
            place = place + bit - 2 * bit * lax.rem(lax.div(place, bit), 2)
        bit *= 2
    return place


def layer_kernel(
    n_rep, n_blk, inv_root,
    slot_ref, x_ref, w_ref, cot_ref, scale_ref, values_ref,
    act_ref, fgrad_ref, wgrad_ref,
    tiles, dense, panel, pair_out, pair_in, line_out, line_in, agg_ref, slope_ref,
    grads, sums, col_out, col_in, w_part, w_in, w_pair_out, w_pair_in, w_line_out, w_line_in,
    tile_sem, feat_sem, pair_sem, line_sem, grad_line_sem, grad_pair_sem, col_sem,
    w_rep_sem, w_pair_sem, w_line_sem,
):
    rep = lax.axis_index("rep")
    blk = lax.axis_index("blk")
    z = lax.div(blk, cores)
    core = lax.rem(blk, cores)
    n_z = n_blk // cores
    cap, side, _ = values_ref.shape
    rows, feat = x_ref.shape
    col_tiles = n_rep * rows // side
    tiles_per_block = rows // side
    f32, bf16 = jnp.float32, jnp.bfloat16
    pair = (rep, blk + 1 - 2 * core)

    def line(mask):
        return flip(z, mask) * cores + core

    pending = []

    def send(source, target, sems, at, device):
        copy = pltpu.make_async_remote_copy(
            src_ref=source, dst_ref=target,
            send_sem=sems.at[0, at], recv_sem=sems.at[1, at],
            device_id=device, device_id_type=MESH,
        )
        copy.start()
        pending.append(copy)
        return copy

    part = cap // load_parts
    loads = []
    for k in range(load_parts):
        piece = pl.ds(k * part, part)
        load = pltpu.make_async_copy(values_ref.at[piece], tiles.at[piece], tile_sem.at[k])
        load.start()
        loads.append(load)
    tiles[cap] = jnp.zeros((side, side), bf16)
    panel[rep] = x_ref[...]

    partners = [(flip(rep, m), blk) for m in range(1, n_rep)]
    partners += [(rep, line(m)) for m in range(1, n_z)]
    partners += [pair]
    barrier = pltpu.get_barrier_semaphore()
    for device in partners:
        pl.semaphore_signal(barrier, inc=1, device_id=device, device_id_type=MESH)
    pl.semaphore_wait(barrier, len(partners))

    feats = [
        send(x_ref, panel.at[rep], feat_sem, m, (flip(rep, m), blk))
        for m in reversed(range(1, n_rep))
    ]
    for load in loads:
        load.wait()

    def place_row(row, carry):
        at = pl.ds(pl.multiple_of(lax.rem(row, tiles_per_block) * side, side), side)
        for col in range(col_tiles):
            slot = slot_ref[row * col_tiles + col]
            dense[lax.div(row, tiles_per_block), at, col * side:(col + 1) * side] = tiles[slot]
        return carry

    lax.fori_loop(0, n_blk * tiles_per_block, place_row, 0)
    for copy in feats:
        copy.wait_recv()

    def forward(block):
        source = panel[...].reshape(n_rep * rows, feat)
        return jnp.dot(dense[block], source, preferred_element_type=f32)

    def pair_step(mask):
        block = flip(z, mask) * cores + 1 - core
        pair_out[mask] = forward(block).astype(bf16)
        return send(pair_out.at[mask], pair_in.at[mask], pair_sem, mask, pair)

    order = list(reversed(range(n_z)))
    pair_copies = {order[0]: pair_step(order[0])}
    line_copies = {}
    own_rows = None
    for at, mask in enumerate(order):
        if at + 1 < n_z:
            pair_copies[order[at + 1]] = pair_step(order[at + 1])
        total = forward(line(mask))
        pair_copies[mask].wait_recv()
        total = total + pair_in[mask].astype(f32)
        if mask:
            line_out[mask] = total.astype(bf16)
            line_copies[mask] = send(
                line_out.at[mask], line_in.at[mask], line_sem, mask, (rep, line(mask))
            )
        else:
            own_rows = total
    for mask in range(1, n_z):
        line_copies[mask].wait_recv()
        own_rows = own_rows + line_in[mask].astype(f32)

    for k in range(tiles_per_block):
        piece = slice(k * side, (k + 1) * side)
        spread = jnp.broadcast_to(scale_ref[:, piece], (feat, side)).T
        agg = (own_rows[piece] + spread * x_ref[piece, :].astype(f32)).astype(bf16)
        agg_ref[piece, :] = agg
        pre_act = jnp.dot(agg, w_ref[...], preferred_element_type=f32)
        sigma = 1.0 / (1.0 + jnp.exp(-pre_act))
        act_ref[piece, :] = (pre_act * sigma).astype(bf16)
        rate = sigma * (1.0 + pre_act * (1.0 - sigma))
        slope = (cot_ref[piece, :].astype(f32) * rate).astype(bf16)
        slope_ref[piece, :] = slope
        grads[blk, :, piece] = lax.dot_general(
            w_ref[...], slope, (((1,), (1,)), ((), ())), preferred_element_type=f32
        ).astype(bf16)

    grad_line = {
        m: send(grads.at[blk], grads.at[blk], grad_line_sem, m, (rep, line(m)))
        for m in reversed(range(1, n_z))
    }
    grad_pair = {0: send(grads.at[blk], grads.at[blk], grad_pair_sem, 0, pair)}

    w_part[...] = jnp.dot(agg_ref[...].T, slope_ref[...], preferred_element_type=f32)
    share = feat // n_rep

    def w_rows(place):
        return pl.ds(pl.multiple_of(place * share, share), share)

    w_rep = [
        send(w_part.at[w_rows(flip(rep, m))], w_in.at[m], w_rep_sem, m, (flip(rep, m), blk))
        for m in range(1, n_rep)
    ]

    def backward(block, first=False):
        for q in range(n_rep):
            term = jnp.dot(
                grads[block], dense[block, :, q * rows:(q + 1) * rows], preferred_element_type=f32
            )
            sums[q] = term if first else sums[q] + term

    backward(blk, True)
    w_pair = None
    w_line = []
    for mask in range(n_z):
        if mask:
            grad_line[mask].wait_recv()
            mine = grads.at[line(mask)]
            grad_pair[mask] = send(mine, mine, grad_pair_sem, mask, pair)
            backward(line(mask))
        if mask == 1:
            for copy in w_rep:
                copy.wait_recv()
            w_sum = w_part[w_rows(rep), :]
            for m in range(1, n_rep):
                w_sum = w_sum + w_in[m]
            w_pair_out[...] = w_sum
            w_pair = send(w_pair_out, w_pair_in, w_pair_sem, 0, pair)
        grad_pair[mask].wait_recv()
        other = flip(z, mask) * cores + 1 - core
        if mask < n_z - 1:
            backward(other)

    w_pair.wait_recv()
    w_line_out[...] = w_pair_out[...] + w_pair_in[...]
    w_line = [
        send(w_line_out, w_line_in.at[m], w_line_sem, m, (rep, line(m))) for m in range(1, n_z)
    ]

    def finished(block):
        at = pl.ds(pl.multiple_of(block * rows, rows), rows)
        return sums[block] + jnp.dot(
            grads[other], dense[other, :, at], preferred_element_type=f32
        )

    col_copies = {}
    for mask in reversed(range(1, n_rep)):
        target = flip(rep, mask)
        col_out[mask] = finished(target).astype(bf16)
        col_copies[mask] = send(
            col_out.at[mask], col_in.at[mask], col_sem, mask, (target, blk)
        )
    own_cols = finished(rep) + scale_ref[...] * grads[blk].astype(f32)

    for copy in w_line:
        copy.wait_recv()
    w_all = w_line_out[...]
    for m in range(1, n_z):
        w_all = w_all + w_line_in[m]
    wgrad_ref[...] = w_all * inv_root

    for mask in range(1, n_rep):
        col_copies[mask].wait_recv()
        own_cols = own_cols + col_in[mask].astype(f32)
    fgrad_ref[...] = own_cols.T.astype(bf16)
    for copy in pending:
        copy.wait_send()


def fused_layer(
    features, weight, cotangent, self_weight, block_rows, block_cols, block_counts, block_values
):
    n_rep = lax.axis_size("rep")
    n_blk = lax.axis_size("blk")
    n_z = n_blk // cores
    _, rows, feat = features.shape
    hidden = weight.shape[1]
    cap, side = block_values.shape[2:4]
    row_tiles = n_blk * rows // side
    col_tiles = n_rep * rows // side
    share = feat // n_rep
    f32, bf16 = jnp.float32, jnp.bfloat16

    slots = jnp.arange(cap, dtype=jnp.int32)
    places = block_rows[0, 0] * col_tiles + block_cols[0, 0]
    places = jnp.where(slots < block_counts[0, 0], places, -1)
    grid = jnp.arange(row_tiles * col_tiles, dtype=jnp.int32)
    slot_of = jnp.min(jnp.where(grid[:, None] == places[None, :], slots[None, :], cap), axis=1)

    vmem = pl.BlockSpec(memory_space=pltpu.VMEM)
    dma = pltpu.SemaphoreType.DMA
    nodes = n_blk * n_rep * rows
    macs = nodes * n_rep * rows * feat // n_rep * 2
    activated, feature_grad, weight_grad = pl.pallas_call(
        functools.partial(layer_kernel, n_rep, n_blk, 1.0 / math.sqrt(nodes)),
        out_shape=(
            jax.ShapeDtypeStruct((rows, hidden), bf16),
            jax.ShapeDtypeStruct((rows, feat), bf16),
            jax.ShapeDtypeStruct((share, hidden), f32),
        ),
        in_specs=[
            pl.BlockSpec(memory_space=pltpu.SMEM), vmem, vmem, vmem, vmem,
            pl.BlockSpec(memory_space=pl.ANY),
        ],
        out_specs=(vmem, vmem, vmem),
        scratch_shapes=[
            pltpu.VMEM((cap + 1, side, side), bf16),
            pltpu.VMEM((n_blk, rows, n_rep * rows), bf16),
            pltpu.VMEM((n_rep, rows, feat), bf16),
            pltpu.VMEM((n_z, rows, feat), bf16),
            pltpu.VMEM((n_z, rows, feat), bf16),
            pltpu.VMEM((n_z, rows, feat), bf16),
            pltpu.VMEM((n_z, rows, feat), bf16),
            pltpu.VMEM((rows, feat), bf16),
            pltpu.VMEM((rows, hidden), bf16),
            pltpu.VMEM((n_blk, feat, rows), bf16),
            pltpu.VMEM((n_rep, feat, rows), f32),
            pltpu.VMEM((n_rep, feat, rows), bf16),
            pltpu.VMEM((n_rep, feat, rows), bf16),
            pltpu.VMEM((feat, hidden), f32),
            pltpu.VMEM((n_rep, share, hidden), f32),
            pltpu.VMEM((share, hidden), f32),
            pltpu.VMEM((share, hidden), f32),
            pltpu.VMEM((share, hidden), f32),
            pltpu.VMEM((n_z, share, hidden), f32),
            dma((load_parts,)),
            dma((2, n_rep)),
            dma((2, n_z)),
            dma((2, n_z)),
            dma((2, n_z)),
            dma((2, n_z)),
            dma((2, n_rep)),
            dma((2, n_rep)),
            dma((2, 1)),
            dma((2, n_z)),
        ],
        compiler_params=pltpu.CompilerParams(
            collective_id=0, has_side_effects=True, vmem_limit_bytes=vmem_bytes
        ),
        cost_estimate=pl.CostEstimate(
            flops=2 * macs, bytes_accessed=cap * side * side * 2, transcendentals=rows * hidden
        ),
    )(slot_of, features[0], weight, cotangent[0], self_weight, block_values[0, 0])
    return (activated[None], feature_grad[None], weight_grad)


def streamed_layer(
    features, weight, cotangent, self_weight, block_rows, block_cols, block_counts, block_values
):
    rows_dev = features.shape[1]
    feat_width = features.shape[2]
    tile_side = block_values.shape[-1]
    blk_count = lax.axis_size("blk")
    rep_count = lax.axis_size("rep")
    tile_values = block_values[0, 0]
    row_index = block_rows[0, 0]
    col_index = block_cols[0, 0]
    live_count = block_counts[0, 0]
    row_tiles = blk_count * rows_dev // tile_side
    col_tiles = rep_count * rows_dev // tile_side
    panel = lax.all_gather(features, "rep", axis=1, tiled=True)
    panel_tiles = panel.reshape(col_tiles, tile_side, feat_width)
    own_scale = self_weight[0][:, None]
    forward_terms = tile_products(
        tile_values, row_index, col_index, live_count, panel_tiles, row_tiles, False
    )
    forward_terms = forward_terms.reshape(blk_count, rows_dev, feat_width)
    summed_rows = lax.psum_scatter(
        forward_terms.astype(jnp.bfloat16), "blk", scatter_dimension=0, tiled=True
    ).astype(jnp.float32)[0]
    aggregated = (summed_rows + own_scale * features[0].astype(jnp.float32)).astype(jnp.bfloat16)
    pre_act = jnp.dot(aggregated, weight, preferred_element_type=jnp.float32)
    activated = jax.nn.silu(pre_act).astype(jnp.bfloat16)
    slope = (cotangent[0].astype(jnp.float32) * silu_slope(pre_act)).astype(jnp.bfloat16)
    node_total = blk_count * rep_count * rows_dev
    weight_part = jnp.einsum(
        "nf,nh->fh", aggregated, slope, preferred_element_type=jnp.float32
    ) / math.sqrt(node_total)
    row_grad = lax.dot_general(
        slope, weight, (((1,), (1,)), ((), ())), preferred_element_type=jnp.float32
    ).astype(jnp.bfloat16)
    all_grads = lax.all_gather(row_grad[None], "blk", axis=0, tiled=True)
    grad_tiles = all_grads.reshape(row_tiles, tile_side, feat_width)
    backward_terms = tile_products(
        tile_values, row_index, col_index, live_count, grad_tiles, col_tiles, True
    )
    backward_terms = backward_terms.reshape(1, rep_count * rows_dev, feat_width)
    own_grad = own_scale * row_grad.astype(jnp.float32)
    column_part = lax.psum_scatter(
        backward_terms.astype(jnp.bfloat16), "rep", scatter_dimension=1, tiled=True
    ).astype(jnp.float32)
    weight_full = lax.psum(weight_part, ("rep", "blk"))
    share_rows = weight_full.shape[0] // rep_count
    weight_grad = lax.dynamic_slice_in_dim(
        weight_full, lax.axis_index("rep") * share_rows, share_rows, 0
    )
    feature_grad = (column_part[0] + own_grad).astype(jnp.bfloat16)
    return (activated[None], feature_grad[None], weight_grad)


def on_device(*arrays):
    n_rep = lax.axis_size("rep")
    n_blk = lax.axis_size("blk")
    rows = arrays[0].shape[1]
    n_z = n_blk // cores
    powers = all(n & (n - 1) == 0 for n in (n_rep, n_z)) and n_z > 1 and n_blk % cores == 0
    dense_bytes = 2 * n_blk * rows * n_rep * rows
    if powers and dense_bytes <= dense_limit:
        return fused_layer(*arrays)
    return streamed_layer(*arrays)


def solution(mesh):
    placed = (
        P("blk", "rep", None),
        P(),
        P("blk", "rep", None),
        P("blk", "rep"),
        P("rep", "blk", None),
        P("rep", "blk", None),
        P("rep", "blk"),
        P("rep", "blk", None, None, None),
    )
    return jax.shard_map(
        on_device,
        mesh=mesh,
        in_specs=placed,
        out_specs=(P("blk", "rep", None), P("blk", "rep", None), P("rep", None)),
        check_vma=False,
    )
```

```python
import functools
import math

import jax
import jax.numpy as jnp
from jax import lax
from jax.experimental import pallas as pl
from jax.experimental.pallas import tpu as pltpu
from jax.sharding import PartitionSpec as P

group_slots = 32


def silu_slope(pre_act):
    sigma = jax.nn.sigmoid(pre_act)
    return sigma * (1.0 + pre_act * (1.0 - sigma))


def tile_products(tile_values, row_index, col_index, live_count, source, targets, flipped):
    feat_width = source.shape[-1]
    tile_side = tile_values.shape[-1]
    start_sums = jnp.zeros((targets, tile_side, feat_width), jnp.float32)
    turn_count = (live_count + group_slots - 1) // group_slots

    def one_group(step_index, summed):
        first_slot = step_index * group_slots
        tile_block = lax.dynamic_slice_in_dim(tile_values, first_slot, group_slots, 0)
        rows_here = lax.dynamic_slice_in_dim(row_index, first_slot, group_slots, 0)
        cols_here = lax.dynamic_slice_in_dim(col_index, first_slot, group_slots, 0)
        is_live = (first_slot + jnp.arange(group_slots, dtype=jnp.int32) < live_count).astype(
            jnp.float32
        )
        if flipped:
            picked = source[rows_here]
            products = jnp.einsum(
                "gji,gjf->gif", tile_block, picked, preferred_element_type=jnp.float32
            )
            landing = cols_here
        else:
            picked = source[cols_here]
            products = jnp.einsum(
                "gij,gjf->gif", tile_block, picked, preferred_element_type=jnp.float32
            )
            landing = rows_here
        return summed.at[landing].add(products * is_live[:, None, None])

    return lax.fori_loop(0, turn_count, one_group, start_sums)


cores = 2
load_parts = 8
halves = 2
near, skip, far = 1, 2, 3
dense_limit = 20 * 2**20
vmem_bytes = 63 * 2**20
MESH = pl.DeviceIdType.MESH


def flip(place, mask):
    bit = 1
    while bit <= mask:
        if mask & bit:
            place = place + bit - 2 * bit * lax.rem(lax.div(place, bit), 2)
        bit *= 2
    return place


def layer_kernel(
    n_rep, n_blk, inv_root,
    slot_ref, x_hbm, w_hbm, cot_hbm, scale_ref, values_ref,
    act_ref, fgrad_ref, wgrad_ref,
    tiles, dense, panel, w_ref, cot_ref, pair_out, pair_in, line_out, line_in, relay_in,
    own_ref, agg_ref, slope_ref, grads, sums, col_out, col_in,
    w_part, w_in, w_pair_out, w_pair_in, w_line_out, w_line_in,
    load_sem, feat_sem, pair_sem, line_sem, grad_line_sem, grad_pair_sem, col_sem,
    w_rep_sem, w_pair_sem, w_line_sem,
):
    rep = lax.axis_index("rep")
    blk = lax.axis_index("blk")
    z = lax.div(blk, cores)
    core = lax.rem(blk, cores)
    n_z = n_blk // cores
    inner = lax.rem(z + lax.div(z, 2), 2) == 1
    end = lax.rem(z + lax.div(z, 2), 2) == 0
    cap, side, _ = values_ref.shape
    _, rows, feat = panel.shape
    half = rows // halves
    col_tiles = n_rep * rows // side
    tiles_per_block = rows // side
    f32, bf16 = jnp.float32, jnp.bfloat16
    pair = (rep, blk + 1 - 2 * core)

    def line(mask):
        return flip(z, mask) * cores + core

    def line_device(mask):
        return (rep, line(mask))

    pending = []

    def ready(source, target, sems, at, device, arrives=None):
        return pltpu.make_async_remote_copy(
            src_ref=source, dst_ref=target,
            send_sem=sems.at[(0,) + at],
            recv_sem=sems.at[(1,) + (at if arrives is None else arrives)],
            device_id=device, device_id_type=MESH,
        )

    def go(copy, only=None):
        if only is None:
            copy.start()
        else:
            pl.when(only)(copy.start)
        pending.append((copy, only))
        return copy

    def send(*args):
        return go(ready(*args))

    x_load = pltpu.make_async_copy(x_hbm, panel.at[rep], load_sem.at[load_parts])
    x_load.start()
    part = cap // load_parts
    loads = []
    for k in range(load_parts):
        piece = pl.ds(k * part, part)
        loads.append(
            pltpu.make_async_copy(values_ref.at[piece], tiles.at[piece], load_sem.at[k])
        )
    loads.append(pltpu.make_async_copy(w_hbm, w_ref, load_sem.at[load_parts + 1]))
    loads.append(pltpu.make_async_copy(cot_hbm, cot_ref, load_sem.at[load_parts + 2]))
    for load in loads:
        load.start()
    tiles[cap] = jnp.zeros((side, side), bf16)

    partners = [(flip(rep, m), blk) for m in range(1, n_rep)]
    partners += [line_device(m) for m in range(1, n_z)]
    partners += [pair]
    barrier = pltpu.get_barrier_semaphore()
    for device in partners:
        pl.semaphore_signal(barrier, inc=1, device_id=device, device_id_type=MESH)
    pl.semaphore_wait(barrier, len(partners))

    x_load.wait()
    feats = [
        send(panel.at[rep], panel.at[rep], feat_sem, (m,), (flip(rep, m), blk))
        for m in reversed(range(1, n_rep))
    ]
    for load in loads:
        load.wait()

    def place_row(row, carry):
        at = pl.ds(pl.multiple_of(lax.rem(row, tiles_per_block) * side, side), side)
        for col in range(col_tiles):
            slot = slot_ref[row * col_tiles + col]
            dense[lax.div(row, tiles_per_block), at, col * side:(col + 1) * side] = tiles[slot]
        return carry

    lax.fori_loop(0, n_blk * tiles_per_block, place_row, 0)
    for copy in feats:
        copy.wait_recv()

    def forward(block, h):
        source = panel[...].reshape(n_rep * rows, feat)
        return jnp.dot(
            dense[block, h * half:(h + 1) * half, :], source, preferred_element_type=f32
        )

    def pair_step(h, mask):
        block = flip(z, mask) * cores + 1 - core
        pair_out[h, mask] = forward(block, h).astype(bf16)
        return send(
            pair_out.at[h, mask], pair_in.at[h, mask], pair_sem, (h, mask), pair
        )

    steps = [(h, mask) for h in range(halves) for mask in (far, near, skip, 0)]
    pair_copies = {steps[0]: pair_step(*steps[0])}
    line_copies = {}
    for at, step in enumerate(steps):
        h, mask = step
        if at + 1 < len(steps):
            pair_copies[steps[at + 1]] = pair_step(*steps[at + 1])
        total = forward(line(mask), h)
        pair_copies[step].wait_recv()
        total = total + pair_in[h, mask].astype(f32)
        if not mask:
            own_ref[h] = total
            continue
        out = line_out.at[h, mask]
        if mask == skip:
            own_ref[h] = total
            relayed = ready(out, relay_in.at[h], line_sem, (h, 0), line_device(near))

            @pl.when(inner)
            def _():
                relayed.wait_recv()
                own_ref[h] = own_ref[h] + relay_in[h].astype(f32)

            total = own_ref[h]
        line_out[h, mask] = total.astype(bf16)
        direct = ready(out, line_in.at[h, mask], line_sem, (h, mask), line_device(mask))
        line_copies[step] = direct
        if mask == far:
            go(direct, inner)
            go(ready(out, relay_in.at[h], line_sem, (h, 0), line_device(near)), end)
        else:
            go(direct)

    def own_layer(h):
        own = own_ref[h]
        for mask in (near, skip):
            line_copies[h, mask].wait_recv()
            own = own + line_in[h, mask].astype(f32)
        own_ref[h] = own

        @pl.when(inner)
        def _():
            line_copies[h, far].wait_recv()
            own_ref[h] = own_ref[h] + line_in[h, far].astype(f32)

        for k in range(half // side):
            inside = slice(k * side, (k + 1) * side)
            piece = slice(h * half + k * side, h * half + (k + 1) * side)
            spread = jnp.broadcast_to(scale_ref[:, piece], (feat, side)).T
            x_piece = panel[rep, piece, :].astype(f32)
            agg = (own_ref[h, inside, :] + spread * x_piece).astype(bf16)
            agg_ref[piece, :] = agg
            pre_act = jnp.dot(agg, w_ref[...], preferred_element_type=f32)
            sigma = 1.0 / (1.0 + jnp.exp(-pre_act))
            act_ref[piece, :] = (pre_act * sigma).astype(bf16)
            rate = sigma * (1.0 + pre_act * (1.0 - sigma))
            slope = (cot_ref[piece, :].astype(f32) * rate).astype(bf16)
            slope_ref[piece, :] = slope
            grads[blk, h, :, inside] = lax.dot_general(
                w_ref[...], slope, (((1,), (1,)), ((), ())), preferred_element_type=f32
            ).astype(bf16)

    grad_line = {}
    grad_pair = {}

    def send_own(h):
        mine = grads.at[blk, h]
        for mask in (skip, far, near):
            copy = ready(mine, mine, grad_line_sem, (h, mask), line_device(mask))
            grad_line[h, mask] = go(copy, inner if mask == far else None)
        grad_pair[h, 0] = send(mine, mine, grad_pair_sem, (h, 0), pair)

    def take(h, mask):
        grad_line[h, mask].wait_recv()
        theirs = grads.at[line(mask), h]
        if mask == skip:
            go(ready(theirs, theirs, grad_line_sem, (h, 0), line_device(near), (h, far)), inner)
        grad_pair[h, mask] = send(theirs, theirs, grad_pair_sem, (h, mask), pair)

    def backward(block, h, first=False):
        for q in range(n_rep):
            term = jnp.dot(
                grads[block, h],
                dense[block, h * half:(h + 1) * half, q * rows:(q + 1) * rows],
                preferred_element_type=f32,
            )
            sums[q] = term if first else sums[q] + term

    def other(mask):
        return flip(z, mask) * cores + 1 - core

    share = feat // n_rep

    def w_rows(place):
        return pl.ds(pl.multiple_of(place * share, share), share)

    for h in range(halves):
        own_layer(h)
        send_own(h)
        piece = slice(h * half, (h + 1) * half)
        term = jnp.dot(agg_ref[piece, :].T, slope_ref[piece, :], preferred_element_type=f32)
        w_part[...] = term if h == 0 else w_part[...] + term
        backward(blk, h, h == 0)
    w_rep = [
        send(w_part.at[w_rows(flip(rep, m))], w_in.at[m], w_rep_sem, (m,), (flip(rep, m), blk))
        for m in range(1, n_rep)
    ]
    for h in range(halves):
        grad_pair[h, 0].wait_recv()
        backward(other(0), h)

    arrivals = [(h, mask) for h in range(halves) for mask in (skip, near, far)]
    for at, (h, mask) in enumerate(arrivals):
        take(h, mask)
        backward(line(mask), h)
        if at == 1:
            for copy in w_rep:
                copy.wait_recv()
            w_sum = w_part[w_rows(rep), :]
            for m in range(1, n_rep):
                w_sum = w_sum + w_in[m]
            w_pair_out[...] = w_sum
            w_pair = send(w_pair_out, w_pair_in, w_pair_sem, (0,), pair)
        grad_pair[h, mask].wait_recv()
        if at + 1 < len(arrivals):
            backward(other(mask), h)

    h, mask = arrivals[-1]
    last = other(mask)

    def finished(block):
        at = pl.ds(pl.multiple_of(block * rows, rows), rows)
        return sums[block] + jnp.dot(
            grads[last, h], dense[last, h * half:(h + 1) * half, at], preferred_element_type=f32
        )

    col_copies = {}
    for mask in reversed(range(1, n_rep)):
        target = flip(rep, mask)
        col_out[mask] = finished(target).astype(bf16)
        col_copies[mask] = send(
            col_out.at[mask], col_in.at[mask], col_sem, (mask,), (target, blk)
        )

    w_pair.wait_recv()
    w_line_out[...] = w_pair_out[...] + w_pair_in[...]
    w_line = [
        send(w_line_out, w_line_in.at[m], w_line_sem, (m,), line_device(m))
        for m in range(1, n_z)
    ]
    own_grads = jnp.concatenate([grads[blk, h] for h in range(halves)], axis=1)
    own_cols = finished(rep) + scale_ref[...] * own_grads.astype(f32)

    for copy in w_line:
        copy.wait_recv()
    w_all = w_line_out[...]
    for m in range(1, n_z):
        w_all = w_all + w_line_in[m]
    wgrad_ref[...] = w_all * inv_root

    for mask in range(1, n_rep):
        col_copies[mask].wait_recv()
        own_cols = own_cols + col_in[mask].astype(f32)
    fgrad_ref[...] = own_cols.T.astype(bf16)
    for copy, only in pending:
        if only is None:
            copy.wait_send()
        else:
            pl.when(only)(copy.wait_send)


def fused_layer(
    features, weight, cotangent, self_weight, block_rows, block_cols, block_counts, block_values
):
    n_rep = lax.axis_size("rep")
    n_blk = lax.axis_size("blk")
    n_z = n_blk // cores
    _, rows, feat = features.shape
    hidden = weight.shape[1]
    cap, side = block_values.shape[2:4]
    row_tiles = n_blk * rows // side
    col_tiles = n_rep * rows // side
    share = feat // n_rep
    f32, bf16 = jnp.float32, jnp.bfloat16

    slots = jnp.arange(cap, dtype=jnp.int32)
    places = block_rows[0, 0] * col_tiles + block_cols[0, 0]
    places = jnp.where(slots < block_counts[0, 0], places, -1)
    grid = jnp.arange(row_tiles * col_tiles, dtype=jnp.int32)
    slot_of = jnp.min(jnp.where(grid[:, None] == places[None, :], slots[None, :], cap), axis=1)

    vmem = pl.BlockSpec(memory_space=pltpu.VMEM)
    hbm = pl.BlockSpec(memory_space=pltpu.HBM)
    half = rows // halves
    dma = pltpu.SemaphoreType.DMA
    nodes = n_blk * n_rep * rows
    macs = nodes * n_rep * rows * feat // n_rep * 2
    activated, feature_grad, weight_grad = pl.pallas_call(
        functools.partial(layer_kernel, n_rep, n_blk, 1.0 / math.sqrt(nodes)),
        out_shape=(
            jax.ShapeDtypeStruct((rows, hidden), bf16),
            jax.ShapeDtypeStruct((rows, feat), bf16),
            jax.ShapeDtypeStruct((share, hidden), f32),
        ),
        in_specs=[
            pl.BlockSpec(memory_space=pltpu.SMEM), hbm, hbm, hbm, vmem, hbm,
        ],
        out_specs=(vmem, vmem, vmem),
        scratch_shapes=[
            pltpu.VMEM((cap + 1, side, side), bf16),
            pltpu.VMEM((n_blk, rows, n_rep * rows), bf16),
            pltpu.VMEM((n_rep, rows, feat), bf16),
            pltpu.VMEM((feat, hidden), bf16),
            pltpu.VMEM((rows, hidden), bf16),
            pltpu.VMEM((halves, n_z, half, feat), bf16),
            pltpu.VMEM((halves, n_z, half, feat), bf16),
            pltpu.VMEM((halves, n_z, half, feat), bf16),
            pltpu.VMEM((halves, n_z, half, feat), bf16),
            pltpu.VMEM((halves, half, feat), bf16),
            pltpu.VMEM((halves, half, feat), f32),
            pltpu.VMEM((rows, feat), bf16),
            pltpu.VMEM((rows, hidden), bf16),
            pltpu.VMEM((n_blk, halves, feat, half), bf16),
            pltpu.VMEM((n_rep, feat, rows), f32),
            pltpu.VMEM((n_rep, feat, rows), bf16),
            pltpu.VMEM((n_rep, feat, rows), bf16),
            pltpu.VMEM((feat, hidden), f32),
            pltpu.VMEM((n_rep, share, hidden), f32),
            pltpu.VMEM((share, hidden), f32),
            pltpu.VMEM((share, hidden), f32),
            pltpu.VMEM((share, hidden), f32),
            pltpu.VMEM((n_z, share, hidden), f32),
            dma((load_parts + 3,)),
            dma((2, n_rep)),
            dma((2, halves, n_z)),
            dma((2, halves, n_z)),
            dma((2, halves, n_z)),
            dma((2, halves, n_z)),
            dma((2, n_rep)),
            dma((2, n_rep)),
            dma((2, 1)),
            dma((2, n_z)),
        ],
        compiler_params=pltpu.CompilerParams(
            collective_id=0, has_side_effects=True, vmem_limit_bytes=vmem_bytes
        ),
        cost_estimate=pl.CostEstimate(
            flops=2 * macs, bytes_accessed=cap * side * side * 2, transcendentals=rows * hidden
        ),
    )(slot_of, features[0], weight, cotangent[0], self_weight, block_values[0, 0])
    return (activated[None], feature_grad[None], weight_grad)


def streamed_layer(
    features, weight, cotangent, self_weight, block_rows, block_cols, block_counts, block_values
):
    rows_dev = features.shape[1]
    feat_width = features.shape[2]
    tile_side = block_values.shape[-1]
    blk_count = lax.axis_size("blk")
    rep_count = lax.axis_size("rep")
    tile_values = block_values[0, 0]
    row_index = block_rows[0, 0]
    col_index = block_cols[0, 0]
    live_count = block_counts[0, 0]
    row_tiles = blk_count * rows_dev // tile_side
    col_tiles = rep_count * rows_dev // tile_side
    panel = lax.all_gather(features, "rep", axis=1, tiled=True)
    panel_tiles = panel.reshape(col_tiles, tile_side, feat_width)
    own_scale = self_weight[0][:, None]
    forward_terms = tile_products(
        tile_values, row_index, col_index, live_count, panel_tiles, row_tiles, False
    )
    forward_terms = forward_terms.reshape(blk_count, rows_dev, feat_width)
    summed_rows = lax.psum_scatter(
        forward_terms.astype(jnp.bfloat16), "blk", scatter_dimension=0, tiled=True
    ).astype(jnp.float32)[0]
    aggregated = (summed_rows + own_scale * features[0].astype(jnp.float32)).astype(jnp.bfloat16)
    pre_act = jnp.dot(aggregated, weight, preferred_element_type=jnp.float32)
    activated = jax.nn.silu(pre_act).astype(jnp.bfloat16)
    slope = (cotangent[0].astype(jnp.float32) * silu_slope(pre_act)).astype(jnp.bfloat16)
    node_total = blk_count * rep_count * rows_dev
    weight_part = jnp.einsum(
        "nf,nh->fh", aggregated, slope, preferred_element_type=jnp.float32
    ) / math.sqrt(node_total)
    row_grad = lax.dot_general(
        slope, weight, (((1,), (1,)), ((), ())), preferred_element_type=jnp.float32
    ).astype(jnp.bfloat16)
    all_grads = lax.all_gather(row_grad[None], "blk", axis=0, tiled=True)
    grad_tiles = all_grads.reshape(row_tiles, tile_side, feat_width)
    backward_terms = tile_products(
        tile_values, row_index, col_index, live_count, grad_tiles, col_tiles, True
    )
    backward_terms = backward_terms.reshape(1, rep_count * rows_dev, feat_width)
    own_grad = own_scale * row_grad.astype(jnp.float32)
    column_part = lax.psum_scatter(
        backward_terms.astype(jnp.bfloat16), "rep", scatter_dimension=1, tiled=True
    ).astype(jnp.float32)
    weight_full = lax.psum(weight_part, ("rep", "blk"))
    share_rows = weight_full.shape[0] // rep_count
    weight_grad = lax.dynamic_slice_in_dim(
        weight_full, lax.axis_index("rep") * share_rows, share_rows, 0
    )
    feature_grad = (column_part[0] + own_grad).astype(jnp.bfloat16)
    return (activated[None], feature_grad[None], weight_grad)


def on_device(*arrays):
    n_rep = lax.axis_size("rep")
    n_blk = lax.axis_size("blk")
    rows = arrays[0].shape[1]
    n_z = n_blk // cores
    fits = n_z == 4 and n_blk % cores == 0 and n_rep & (n_rep - 1) == 0
    dense_bytes = 2 * n_blk * rows * n_rep * rows
    if fits and dense_bytes <= dense_limit:
        return fused_layer(*arrays)
    return streamed_layer(*arrays)


def solution(mesh):
    placed = (
        P("blk", "rep", None),
        P(),
        P("blk", "rep", None),
        P("blk", "rep"),
        P("rep", "blk", None),
        P("rep", "blk", None),
        P("rep", "blk"),
        P("rep", "blk", None, None, None),
    )
    return jax.shard_map(
        on_device,
        mesh=mesh,
        in_specs=placed,
        out_specs=(P("blk", "rep", None), P("blk", "rep", None), P("rep", None)),
        check_vma=False,
    )
```

```python
import functools
import math

import jax
import jax.numpy as jnp
from jax import lax
from jax.experimental import pallas as pl
from jax.experimental.pallas import tpu as pltpu
from jax.sharding import PartitionSpec as P

group_slots = 32


def silu_slope(pre_act):
    sigma = jax.nn.sigmoid(pre_act)
    return sigma * (1.0 + pre_act * (1.0 - sigma))


def tile_products(tile_values, row_index, col_index, live_count, source, targets, flipped):
    feat_width = source.shape[-1]
    tile_side = tile_values.shape[-1]
    start_sums = jnp.zeros((targets, tile_side, feat_width), jnp.float32)
    turn_count = (live_count + group_slots - 1) // group_slots

    def one_group(step_index, summed):
        first_slot = step_index * group_slots
        tile_block = lax.dynamic_slice_in_dim(tile_values, first_slot, group_slots, 0)
        rows_here = lax.dynamic_slice_in_dim(row_index, first_slot, group_slots, 0)
        cols_here = lax.dynamic_slice_in_dim(col_index, first_slot, group_slots, 0)
        is_live = (first_slot + jnp.arange(group_slots, dtype=jnp.int32) < live_count).astype(
            jnp.float32
        )
        if flipped:
            picked = source[rows_here]
            products = jnp.einsum(
                "gji,gjf->gif", tile_block, picked, preferred_element_type=jnp.float32
            )
            landing = cols_here
        else:
            picked = source[cols_here]
            products = jnp.einsum(
                "gij,gjf->gif", tile_block, picked, preferred_element_type=jnp.float32
            )
            landing = rows_here
        return summed.at[landing].add(products * is_live[:, None, None])

    return lax.fori_loop(0, turn_count, one_group, start_sums)


cores = 2
load_parts = 8
halves = 2
near, skip, far = 1, 2, 3
dense_limit = 20 * 2**20
vmem_bytes = 63 * 2**20
MESH = pl.DeviceIdType.MESH


def flip(place, mask):
    bit = 1
    while bit <= mask:
        if mask & bit:
            place = place + bit - 2 * bit * lax.rem(lax.div(place, bit), 2)
        bit *= 2
    return place


def layer_kernel(
    n_rep, n_blk, inv_root,
    rows_ref, cols_ref, count_ref, x_hbm, w_hbm, cot_hbm, scale_ref, values_ref,
    act_ref, fgrad_ref, wgrad_ref,
    slot_map, slot_ref, tiles, dense, panel, w_ref, cot_ref, pair_out, pair_in, line_out, line_in, relay_in,
    own_ref, agg_ref, slope_ref, grads, sums, col_out, col_in,
    w_part, w_in, w_pair_out, w_pair_in, w_line_out, w_line_in,
    load_sem, feat_sem, pair_sem, line_sem, grad_line_sem, grad_pair_sem, col_sem,
    w_rep_sem, w_pair_sem, w_line_sem,
):
    rep = lax.axis_index("rep")
    blk = lax.axis_index("blk")
    z = lax.div(blk, cores)
    core = lax.rem(blk, cores)
    n_z = n_blk // cores
    inner = lax.rem(z + lax.div(z, 2), 2) == 1
    end = lax.rem(z + lax.div(z, 2), 2) == 0
    cap, side, _ = values_ref.shape
    _, rows, feat = panel.shape
    half = rows // halves
    col_tiles = n_rep * rows // side
    tiles_per_block = rows // side
    f32, bf16 = jnp.float32, jnp.bfloat16
    pair = (rep, blk + 1 - 2 * core)

    def line(mask):
        return flip(z, mask) * cores + core

    def line_device(mask):
        return (rep, line(mask))

    pending = []

    def ready(source, target, sems, at, device, arrives=None):
        return pltpu.make_async_remote_copy(
            src_ref=source, dst_ref=target,
            send_sem=sems.at[(0,) + at],
            recv_sem=sems.at[(1,) + (at if arrives is None else arrives)],
            device_id=device, device_id_type=MESH,
        )

    def go(copy, only=None):
        if only is None:
            copy.start()
        else:
            pl.when(only)(copy.start)
        pending.append((copy, only))
        return copy

    def send(*args):
        return go(ready(*args))

    x_load = pltpu.make_async_copy(x_hbm, panel.at[rep], load_sem.at[load_parts])
    x_load.start()
    part = cap // load_parts
    loads = []
    for k in range(load_parts):
        piece = pl.ds(k * part, part)
        loads.append(
            pltpu.make_async_copy(values_ref.at[piece], tiles.at[piece], load_sem.at[k])
        )
    loads.append(pltpu.make_async_copy(w_hbm, w_ref, load_sem.at[load_parts + 1]))
    loads.append(pltpu.make_async_copy(cot_hbm, cot_ref, load_sem.at[load_parts + 2]))
    for load in loads:
        load.start()
    tiles[cap] = jnp.zeros((side, side), bf16)

    partners = [(flip(rep, m), blk) for m in range(1, n_rep)]
    partners += [line_device(m) for m in range(1, n_z)]
    partners += [pair]
    barrier = pltpu.get_barrier_semaphore()
    for device in partners:
        pl.semaphore_signal(barrier, inc=1, device_id=device, device_id_type=MESH)
    pl.semaphore_wait(barrier, len(partners))

    x_load.wait()
    feats = [
        send(panel.at[rep], panel.at[rep], feat_sem, (m,), (flip(rep, m), blk))
        for m in reversed(range(1, n_rep))
    ]

    lanes = slot_map.shape[1]
    places = lax.broadcasted_iota(jnp.int32, slot_map.shape, 0) * lanes
    places = places + lax.broadcasted_iota(jnp.int32, slot_map.shape, 1)
    count = count_ref[0, 0]

    def name_place(slot, named):
        place = rows_ref[0, slot] * col_tiles + cols_ref[0, slot]
        place = jnp.where(slot < count, place, -1)
        return jnp.where(places == place, slot, named)

    slot_map[...] = lax.fori_loop(
        0, cap, name_place, jnp.full(slot_map.shape, cap, jnp.int32), unroll=8
    )
    map_copy = pltpu.make_async_copy(slot_map, slot_ref, load_sem.at[load_parts + 3])
    map_copy.start()
    map_copy.wait()
    for load in loads:
        load.wait()

    def place(block, h):
        def place_row(k, carry):
            first = (block * tiles_per_block + h * (half // side) + k) * col_tiles
            at = pl.ds(pl.multiple_of(h * half + k * side, side), side)
            for col in range(col_tiles):
                slot = slot_ref[lax.div(first, lanes), lax.rem(first, lanes) + col]
                dense[block, at, col * side:(col + 1) * side] = tiles[slot]
            return carry

        lax.fori_loop(0, half // side, place_row, 0)

    def place_block(block, carry):
        place(block, 0)
        return carry

    lax.fori_loop(0, n_blk, place_block, 0)
    for copy in feats:
        copy.wait_recv()

    def forward(block, h):
        if h:
            place(block, h)
        source = panel[...].reshape(n_rep * rows, feat)
        return jnp.dot(
            dense[block, h * half:(h + 1) * half, :], source, preferred_element_type=f32
        )

    def pair_step(h, mask):
        block = flip(z, mask) * cores + 1 - core
        pair_out[h, mask] = forward(block, h).astype(bf16)
        return send(
            pair_out.at[h, mask], pair_in.at[h, mask], pair_sem, (h, mask), pair
        )

    steps = [(h, mask) for h in range(halves) for mask in (far, near, skip, 0)]
    pair_copies = {steps[0]: pair_step(*steps[0])}
    line_copies = {}
    for at, step in enumerate(steps):
        h, mask = step
        if at + 1 < len(steps):
            pair_copies[steps[at + 1]] = pair_step(*steps[at + 1])
        total = forward(line(mask), h)
        pair_copies[step].wait_recv()
        total = total + pair_in[h, mask].astype(f32)
        if not mask:
            own_ref[h] = total
            continue
        out = line_out.at[h, mask]
        if mask == skip:
            own_ref[h] = total
            relayed = ready(out, relay_in.at[h], line_sem, (h, 0), line_device(near))

            @pl.when(inner)
            def _():
                relayed.wait_recv()
                own_ref[h] = own_ref[h] + relay_in[h].astype(f32)

            total = own_ref[h]
        line_out[h, mask] = total.astype(bf16)
        direct = ready(out, line_in.at[h, mask], line_sem, (h, mask), line_device(mask))
        line_copies[step] = direct
        if mask == far:
            go(direct, inner)
            go(ready(out, relay_in.at[h], line_sem, (h, 0), line_device(near)), end)
        else:
            go(direct)

    def own_layer(h):
        own = own_ref[h]
        for mask in (near, skip):
            line_copies[h, mask].wait_recv()
            own = own + line_in[h, mask].astype(f32)
        own_ref[h] = own

        @pl.when(inner)
        def _():
            line_copies[h, far].wait_recv()
            own_ref[h] = own_ref[h] + line_in[h, far].astype(f32)

        for k in range(half // side):
            inside = slice(k * side, (k + 1) * side)
            piece = slice(h * half + k * side, h * half + (k + 1) * side)
            spread = jnp.broadcast_to(scale_ref[:, piece], (feat, side)).T
            x_piece = panel[rep, piece, :].astype(f32)
            agg = (own_ref[h, inside, :] + spread * x_piece).astype(bf16)
            agg_ref[piece, :] = agg
            pre_act = jnp.dot(agg, w_ref[...], preferred_element_type=f32)
            sigma = 1.0 / (1.0 + jnp.exp(-pre_act))
            act_ref[piece, :] = (pre_act * sigma).astype(bf16)
            rate = sigma * (1.0 + pre_act * (1.0 - sigma))
            slope = (cot_ref[piece, :].astype(f32) * rate).astype(bf16)
            slope_ref[piece, :] = slope
            grads[blk, h, :, inside] = lax.dot_general(
                w_ref[...], slope, (((1,), (1,)), ((), ())), preferred_element_type=f32
            ).astype(bf16)

    grad_line = {}
    grad_pair = {}

    def send_own(h):
        mine = grads.at[blk, h]
        for mask in (skip, far, near):
            copy = ready(mine, mine, grad_line_sem, (h, mask), line_device(mask))
            grad_line[h, mask] = go(copy, inner if mask == far else None)
        grad_pair[h, 0] = send(mine, mine, grad_pair_sem, (h, 0), pair)

    def take(h, mask):
        grad_line[h, mask].wait_recv()
        theirs = grads.at[line(mask), h]
        if mask == skip:
            go(ready(theirs, theirs, grad_line_sem, (h, 0), line_device(near), (h, far)), inner)
        grad_pair[h, mask] = send(theirs, theirs, grad_pair_sem, (h, mask), pair)

    def backward(block, h, first=False):
        for q in range(n_rep):
            term = jnp.dot(
                grads[block, h],
                dense[block, h * half:(h + 1) * half, q * rows:(q + 1) * rows],
                preferred_element_type=f32,
            )
            sums[q] = term if first else sums[q] + term

    def other(mask):
        return flip(z, mask) * cores + 1 - core

    share = feat // n_rep

    def w_rows(place):
        return pl.ds(pl.multiple_of(place * share, share), share)

    for h in range(halves):
        own_layer(h)
        send_own(h)
        piece = slice(h * half, (h + 1) * half)
        term = jnp.dot(agg_ref[piece, :].T, slope_ref[piece, :], preferred_element_type=f32)
        w_part[...] = term if h == 0 else w_part[...] + term
        backward(blk, h, h == 0)
    w_rep = [
        send(w_part.at[w_rows(flip(rep, m))], w_in.at[m], w_rep_sem, (m,), (flip(rep, m), blk))
        for m in range(1, n_rep)
    ]
    for h in range(halves):
        grad_pair[h, 0].wait_recv()
        backward(other(0), h)

    arrivals = [(h, mask) for h in range(halves) for mask in (skip, near, far)]
    for at, (h, mask) in enumerate(arrivals):
        take(h, mask)
        backward(line(mask), h)
        if at == 1:
            for copy in w_rep:
                copy.wait_recv()
            w_sum = w_part[w_rows(rep), :]
            for m in range(1, n_rep):
                w_sum = w_sum + w_in[m]
            w_pair_out[...] = w_sum
            w_pair = send(w_pair_out, w_pair_in, w_pair_sem, (0,), pair)
        grad_pair[h, mask].wait_recv()
        if at + 1 < len(arrivals):
            backward(other(mask), h)

    h, mask = arrivals[-1]
    last = other(mask)

    def finished(block):
        at = pl.ds(pl.multiple_of(block * rows, rows), rows)
        return sums[block] + jnp.dot(
            grads[last, h], dense[last, h * half:(h + 1) * half, at], preferred_element_type=f32
        )

    col_copies = {}
    for mask in reversed(range(1, n_rep)):
        target = flip(rep, mask)
        col_out[mask] = finished(target).astype(bf16)
        col_copies[mask] = send(
            col_out.at[mask], col_in.at[mask], col_sem, (mask,), (target, blk)
        )

    w_pair.wait_recv()
    w_line_out[...] = w_pair_out[...] + w_pair_in[...]
    w_line = [
        send(w_line_out, w_line_in.at[m], w_line_sem, (m,), line_device(m))
        for m in range(1, n_z)
    ]
    own_grads = jnp.concatenate([grads[blk, h] for h in range(halves)], axis=1)
    own_cols = finished(rep) + scale_ref[...] * own_grads.astype(f32)

    for copy in w_line:
        copy.wait_recv()
    w_all = w_line_out[...]
    for m in range(1, n_z):
        w_all = w_all + w_line_in[m]
    wgrad_ref[...] = w_all * inv_root

    for mask in range(1, n_rep):
        col_copies[mask].wait_recv()
        own_cols = own_cols + col_in[mask].astype(f32)
    fgrad_ref[...] = own_cols.T.astype(bf16)
    for copy, only in pending:
        if only is None:
            copy.wait_send()
        else:
            pl.when(only)(copy.wait_send)


def hand_over(a_ref, b_ref, c_ref, a_out, b_out, c_out, sems):
    pairs = ((a_ref, a_out), (b_ref, b_out), (c_ref, c_out))
    copies = [pltpu.make_async_copy(p, q, sems.at[k]) for k, (p, q) in enumerate(pairs)]
    for copy in copies:
        copy.start()
    for copy in copies:
        copy.wait()


def fused_layer(
    features, weight, cotangent, self_weight, block_rows, block_cols, block_counts, block_values
):
    n_rep = lax.axis_size("rep")
    n_blk = lax.axis_size("blk")
    n_z = n_blk // cores
    _, rows, feat = features.shape
    hidden = weight.shape[1]
    cap, side = block_values.shape[2:4]
    row_tiles = n_blk * rows // side
    col_tiles = n_rep * rows // side
    share = feat // n_rep
    f32, bf16 = jnp.float32, jnp.bfloat16

    map_lanes = 128
    map_rows = row_tiles * col_tiles // map_lanes
    vmem = pl.BlockSpec(memory_space=pltpu.VMEM)
    hbm = pl.BlockSpec(memory_space=pltpu.HBM)
    smem = pl.BlockSpec(memory_space=pltpu.SMEM)
    half = rows // halves
    dma = pltpu.SemaphoreType.DMA
    nodes = n_blk * n_rep * rows
    macs = nodes * n_rep * rows * feat // n_rep * 2
    activated, feature_grad, weight_grad = pl.pallas_call(
        functools.partial(layer_kernel, n_rep, n_blk, 1.0 / math.sqrt(nodes)),
        out_shape=(
            jax.ShapeDtypeStruct((rows, hidden), bf16),
            jax.ShapeDtypeStruct((rows, feat), bf16),
            jax.ShapeDtypeStruct((share, hidden), f32),
        ),
        in_specs=[
            smem, smem, smem, hbm, hbm, hbm, vmem, hbm,
        ],
        out_specs=(vmem, vmem, vmem),
        scratch_shapes=[
            pltpu.VMEM((map_rows, map_lanes), jnp.int32),
            pltpu.SMEM((map_rows, map_lanes), jnp.int32),
            pltpu.VMEM((cap + 1, side, side), bf16),
            pltpu.VMEM((n_blk, rows, n_rep * rows), bf16),
            pltpu.VMEM((n_rep, rows, feat), bf16),
            pltpu.VMEM((feat, hidden), bf16),
            pltpu.VMEM((rows, hidden), bf16),
            pltpu.VMEM((halves, n_z, half, feat), bf16),
            pltpu.VMEM((halves, n_z, half, feat), bf16),
            pltpu.VMEM((halves, n_z, half, feat), bf16),
            pltpu.VMEM((halves, n_z, half, feat), bf16),
            pltpu.VMEM((halves, half, feat), bf16),
            pltpu.VMEM((halves, half, feat), f32),
            pltpu.VMEM((rows, feat), bf16),
            pltpu.VMEM((rows, hidden), bf16),
            pltpu.VMEM((n_blk, halves, feat, half), bf16),
            pltpu.VMEM((n_rep, feat, rows), f32),
            pltpu.VMEM((n_rep, feat, rows), bf16),
            pltpu.VMEM((n_rep, feat, rows), bf16),
            pltpu.VMEM((feat, hidden), f32),
            pltpu.VMEM((n_rep, share, hidden), f32),
            pltpu.VMEM((share, hidden), f32),
            pltpu.VMEM((share, hidden), f32),
            pltpu.VMEM((share, hidden), f32),
            pltpu.VMEM((n_z, share, hidden), f32),
            dma((load_parts + 4,)),
            dma((2, n_rep)),
            dma((2, halves, n_z)),
            dma((2, halves, n_z)),
            dma((2, halves, n_z)),
            dma((2, halves, n_z)),
            dma((2, n_rep)),
            dma((2, n_rep)),
            dma((2, 1)),
            dma((2, n_z)),
        ],
        compiler_params=pltpu.CompilerParams(
            collective_id=0, has_side_effects=True, vmem_limit_bytes=vmem_bytes
        ),
        cost_estimate=pl.CostEstimate(
            flops=2 * macs, bytes_accessed=cap * side * side * 2, transcendentals=rows * hidden
        ),
    )(
        block_rows[0], block_cols[0], block_counts,
        features[0], weight, cotangent[0], self_weight, block_values[0, 0],
    )
    results = (activated[None], feature_grad[None], weight_grad)
    return pl.pallas_call(
        hand_over,
        out_shape=tuple(jax.ShapeDtypeStruct(r.shape, r.dtype) for r in results),
        in_specs=[hbm] * 3,
        out_specs=(hbm,) * 3,
        scratch_shapes=[dma((3,))],
        compiler_params=pltpu.CompilerParams(vmem_limit_bytes=vmem_bytes),
    )(*results)


def streamed_layer(
    features, weight, cotangent, self_weight, block_rows, block_cols, block_counts, block_values
):
    rows_dev = features.shape[1]
    feat_width = features.shape[2]
    tile_side = block_values.shape[-1]
    blk_count = lax.axis_size("blk")
    rep_count = lax.axis_size("rep")
    tile_values = block_values[0, 0]
    row_index = block_rows[0, 0]
    col_index = block_cols[0, 0]
    live_count = block_counts[0, 0]
    row_tiles = blk_count * rows_dev // tile_side
    col_tiles = rep_count * rows_dev // tile_side
    panel = lax.all_gather(features, "rep", axis=1, tiled=True)
    panel_tiles = panel.reshape(col_tiles, tile_side, feat_width)
    own_scale = self_weight[0][:, None]
    forward_terms = tile_products(
        tile_values, row_index, col_index, live_count, panel_tiles, row_tiles, False
    )
    forward_terms = forward_terms.reshape(blk_count, rows_dev, feat_width)
    summed_rows = lax.psum_scatter(
        forward_terms.astype(jnp.bfloat16), "blk", scatter_dimension=0, tiled=True
    ).astype(jnp.float32)[0]
    aggregated = (summed_rows + own_scale * features[0].astype(jnp.float32)).astype(jnp.bfloat16)
    pre_act = jnp.dot(aggregated, weight, preferred_element_type=jnp.float32)
    activated = jax.nn.silu(pre_act).astype(jnp.bfloat16)
    slope = (cotangent[0].astype(jnp.float32) * silu_slope(pre_act)).astype(jnp.bfloat16)
    node_total = blk_count * rep_count * rows_dev
    weight_part = jnp.einsum(
        "nf,nh->fh", aggregated, slope, preferred_element_type=jnp.float32
    ) / math.sqrt(node_total)
    row_grad = lax.dot_general(
        slope, weight, (((1,), (1,)), ((), ())), preferred_element_type=jnp.float32
    ).astype(jnp.bfloat16)
    all_grads = lax.all_gather(row_grad[None], "blk", axis=0, tiled=True)
    grad_tiles = all_grads.reshape(row_tiles, tile_side, feat_width)
    backward_terms = tile_products(
        tile_values, row_index, col_index, live_count, grad_tiles, col_tiles, True
    )
    backward_terms = backward_terms.reshape(1, rep_count * rows_dev, feat_width)
    own_grad = own_scale * row_grad.astype(jnp.float32)
    column_part = lax.psum_scatter(
        backward_terms.astype(jnp.bfloat16), "rep", scatter_dimension=1, tiled=True
    ).astype(jnp.float32)
    weight_full = lax.psum(weight_part, ("rep", "blk"))
    share_rows = weight_full.shape[0] // rep_count
    weight_grad = lax.dynamic_slice_in_dim(
        weight_full, lax.axis_index("rep") * share_rows, share_rows, 0
    )
    feature_grad = (column_part[0] + own_grad).astype(jnp.bfloat16)
    return (activated[None], feature_grad[None], weight_grad)


def on_device(*arrays):
    n_rep = lax.axis_size("rep")
    n_blk = lax.axis_size("blk")
    rows = arrays[0].shape[1]
    n_z = n_blk // cores
    fits = n_z == 4 and n_blk % cores == 0 and n_rep & (n_rep - 1) == 0
    side = arrays[-1].shape[-1]
    fits = fits and 128 % (n_rep * rows // side) == 0
    dense_bytes = 2 * n_blk * rows * n_rep * rows
    if fits and dense_bytes <= dense_limit:
        return fused_layer(*arrays)
    return streamed_layer(*arrays)


def solution(mesh):
    placed = (
        P("blk", "rep", None),
        P(),
        P("blk", "rep", None),
        P("blk", "rep"),
        P("rep", "blk", None),
        P("rep", "blk", None),
        P("rep", "blk"),
        P("rep", "blk", None, None, None),
    )
    return jax.shard_map(
        on_device,
        mesh=mesh,
        in_specs=placed,
        out_specs=(P("blk", "rep", None), P("blk", "rep", None), P("rep", None)),
        check_vma=False,
    )
```

```python
import functools
import math

import jax
import jax.numpy as jnp
from jax import lax
from jax.experimental import pallas as pl
from jax.experimental.pallas import tpu as pltpu
from jax.sharding import PartitionSpec as P

group_slots = 32


def silu_slope(pre_act):
    sigma = jax.nn.sigmoid(pre_act)
    return sigma * (1.0 + pre_act * (1.0 - sigma))


def tile_products(tile_values, row_index, col_index, live_count, source, targets, flipped):
    feat_width = source.shape[-1]
    tile_side = tile_values.shape[-1]
    start_sums = jnp.zeros((targets, tile_side, feat_width), jnp.float32)
    turn_count = (live_count + group_slots - 1) // group_slots

    def one_group(step_index, summed):
        first_slot = step_index * group_slots
        tile_block = lax.dynamic_slice_in_dim(tile_values, first_slot, group_slots, 0)
        rows_here = lax.dynamic_slice_in_dim(row_index, first_slot, group_slots, 0)
        cols_here = lax.dynamic_slice_in_dim(col_index, first_slot, group_slots, 0)
        is_live = (first_slot + jnp.arange(group_slots, dtype=jnp.int32) < live_count).astype(
            jnp.float32
        )
        if flipped:
            picked = source[rows_here]
            products = jnp.einsum(
                "gji,gjf->gif", tile_block, picked, preferred_element_type=jnp.float32
            )
            landing = cols_here
        else:
            picked = source[cols_here]
            products = jnp.einsum(
                "gij,gjf->gif", tile_block, picked, preferred_element_type=jnp.float32
            )
            landing = rows_here
        return summed.at[landing].add(products * is_live[:, None, None])

    return lax.fori_loop(0, turn_count, one_group, start_sums)


cores = 2
load_parts = 8
halves = 2
near, skip, far = 1, 2, 3
dense_limit = 20 * 2**20
vmem_bytes = 60 * 2**20
MESH = pl.DeviceIdType.MESH


def flip(place, mask):
    bit = 1
    while bit <= mask:
        if mask & bit:
            place = place + bit - 2 * bit * lax.rem(lax.div(place, bit), 2)
        bit *= 2
    return place


def layer_kernel(
    n_rep, n_blk, inv_root,
    rows_ref, cols_ref, count_ref, x_hbm, w_hbm, cot_hbm, scale_ref, values_ref,
    act_ref, fgrad_ref, wgrad_ref,
    slot_map, slot_ref, tiles, dense, panel, w_ref, cot_ref, pair_out, pair_in, line_out, line_in, relay_in,
    own_ref, agg_ref, slope_ref, grads, sums, col_out, col_in,
    w_part, w_in, w_pair_out, w_pair_in, w_line_out, w_line_in,
    load_sem, feat_sem, pair_sem, line_sem, grad_line_sem, grad_pair_sem, col_sem,
    w_rep_sem, w_pair_sem, w_line_sem,
):
    rep = lax.axis_index("rep")
    blk = lax.axis_index("blk")
    z = lax.div(blk, cores)
    core = lax.rem(blk, cores)
    n_z = n_blk // cores
    inner = lax.rem(z + lax.div(z, 2), 2) == 1
    end = lax.rem(z + lax.div(z, 2), 2) == 0
    cap, side, _ = values_ref.shape
    _, rows, feat = panel.shape
    half = rows // halves
    col_tiles = n_rep * rows // side
    tiles_per_block = rows // side
    f32, bf16 = jnp.float32, jnp.bfloat16
    pair = (rep, blk + 1 - 2 * core)

    def line(mask):
        return flip(z, mask) * cores + core

    def line_device(mask):
        return (rep, line(mask))

    pending = []

    def ready(source, target, sems, at, device, arrives=None):
        return pltpu.make_async_remote_copy(
            src_ref=source, dst_ref=target,
            send_sem=sems.at[(0,) + at],
            recv_sem=sems.at[(1,) + (at if arrives is None else arrives)],
            device_id=device, device_id_type=MESH,
        )

    def go(copy, only=None):
        if only is None:
            copy.start()
        else:
            pl.when(only)(copy.start)
        pending.append((copy, only))
        return copy

    def send(*args):
        return go(ready(*args))

    x_load = pltpu.make_async_copy(x_hbm, panel.at[rep], load_sem.at[load_parts])
    x_load.start()
    part = cap // load_parts
    loads = []
    for k in range(load_parts):
        piece = pl.ds(k * part, part)
        loads.append(
            pltpu.make_async_copy(values_ref.at[piece], tiles.at[piece], load_sem.at[k])
        )
    loads.append(pltpu.make_async_copy(w_hbm, w_ref, load_sem.at[load_parts + 1]))
    loads.append(pltpu.make_async_copy(cot_hbm, cot_ref, load_sem.at[load_parts + 2]))
    for load in loads:
        load.start()
    tiles[cap] = jnp.zeros((side, side), bf16)

    partners = [(flip(rep, m), blk) for m in range(1, n_rep)]
    partners += [line_device(m) for m in range(1, n_z)]
    partners += [pair]
    barrier = pltpu.get_barrier_semaphore()
    for device in partners:
        pl.semaphore_signal(barrier, inc=1, device_id=device, device_id_type=MESH)
    pl.semaphore_wait(barrier, len(partners))

    x_load.wait()
    feats = [
        send(panel.at[rep], panel.at[rep], feat_sem, (m,), (flip(rep, m), blk))
        for m in reversed(range(1, n_rep))
    ]

    lanes = slot_map.shape[1]
    places = lax.broadcasted_iota(jnp.int32, slot_map.shape, 0) * lanes
    places = places + lax.broadcasted_iota(jnp.int32, slot_map.shape, 1)
    count = count_ref[0, 0]

    def name_place(slot, named):
        place = rows_ref[0, slot] * col_tiles + cols_ref[0, slot]
        place = jnp.where(slot < count, place, -1)
        return jnp.where(places == place, slot, named)

    slot_map[...] = lax.fori_loop(
        0, cap, name_place, jnp.full(slot_map.shape, cap, jnp.int32), unroll=8
    )
    map_copy = pltpu.make_async_copy(slot_map, slot_ref, load_sem.at[load_parts + 3])
    map_copy.start()
    map_copy.wait()
    for load in loads:
        load.wait()

    def place(block, h):
        def place_row(k, carry):
            first = (block * tiles_per_block + h * (half // side) + k) * col_tiles
            at = pl.ds(pl.multiple_of(h * half + k * side, side), side)
            for col in range(col_tiles):
                slot = slot_ref[lax.div(first, lanes), lax.rem(first, lanes) + col]
                dense[block, at, col * side:(col + 1) * side] = tiles[slot]
            return carry

        lax.fori_loop(0, half // side, place_row, 0)

    def place_block(block, carry):
        place(block, 0)
        return carry

    lax.fori_loop(0, n_blk, place_block, 0)
    for copy in feats:
        copy.wait_recv()

    def forward(block, h):
        if h:
            place(block, h)
        source = panel[...].reshape(n_rep * rows, feat)
        return jnp.dot(
            dense[block, h * half:(h + 1) * half, :], source, preferred_element_type=f32
        )

    def pair_step(h, mask):
        block = flip(z, mask) * cores + 1 - core
        pair_out[h, mask] = forward(block, h).astype(bf16)
        return send(
            pair_out.at[h, mask], pair_in.at[h, mask], pair_sem, (h, mask), pair
        )

    steps = [(h, mask) for h in range(halves) for mask in (far, near, skip, 0)]
    pair_copies = {steps[0]: pair_step(*steps[0])}
    line_copies = {}
    for at, step in enumerate(steps):
        h, mask = step
        if at + 1 < len(steps):
            pair_copies[steps[at + 1]] = pair_step(*steps[at + 1])
        total = forward(line(mask), h)
        pair_copies[step].wait_recv()
        total = total + pair_in[h, mask].astype(f32)
        if not mask:
            own_ref[h] = total
            continue
        out = line_out.at[h, mask]
        if mask == skip:
            own_ref[h] = total
            relayed = ready(out, relay_in.at[h], line_sem, (h, 0), line_device(near))

            @pl.when(inner)
            def _():
                relayed.wait_recv()
                own_ref[h] = own_ref[h] + relay_in[h].astype(f32)

            total = own_ref[h]
        line_out[h, mask] = total.astype(bf16)
        direct = ready(out, line_in.at[h, mask], line_sem, (h, mask), line_device(mask))
        line_copies[step] = direct
        if mask == far:
            go(direct, inner)
            go(ready(out, relay_in.at[h], line_sem, (h, 0), line_device(near)), end)
        else:
            go(direct)

    def own_layer(h):
        own = own_ref[h]
        for mask in (near, skip):
            line_copies[h, mask].wait_recv()
            own = own + line_in[h, mask].astype(f32)
        own_ref[h] = own

        @pl.when(inner)
        def _():
            line_copies[h, far].wait_recv()
            own_ref[h] = own_ref[h] + line_in[h, far].astype(f32)

        for k in range(half // side):
            inside = slice(k * side, (k + 1) * side)
            piece = slice(h * half + k * side, h * half + (k + 1) * side)
            spread = jnp.broadcast_to(scale_ref[:, piece], (feat, side)).T
            x_piece = panel[rep, piece, :].astype(f32)
            agg = (own_ref[h, inside, :] + spread * x_piece).astype(bf16)
            agg_ref[piece, :] = agg
            pre_act = jnp.dot(agg, w_ref[...], preferred_element_type=f32)
            sigma = 1.0 / (1.0 + jnp.exp(-pre_act))
            act_ref[piece, :] = (pre_act * sigma).astype(bf16)
            rate = sigma * (1.0 + pre_act * (1.0 - sigma))
            slope = (cot_ref[piece, :].astype(f32) * rate).astype(bf16)
            slope_ref[piece, :] = slope
            grads[blk, h, :, inside] = lax.dot_general(
                w_ref[...], slope, (((1,), (1,)), ((), ())), preferred_element_type=f32
            ).astype(bf16)

    grad_line = {}
    grad_pair = {}

    def send_own(h):
        mine = grads.at[blk, h]
        for mask in (skip, far, near):
            copy = ready(mine, mine, grad_line_sem, (h, mask), line_device(mask))
            grad_line[h, mask] = go(copy, inner if mask == far else None)
        grad_pair[h, 0] = send(mine, mine, grad_pair_sem, (h, 0), pair)

    def take(h, mask):
        grad_line[h, mask].wait_recv()
        theirs = grads.at[line(mask), h]
        if mask == skip:
            go(ready(theirs, theirs, grad_line_sem, (h, 0), line_device(near), (h, far)), inner)
        grad_pair[h, mask] = send(theirs, theirs, grad_pair_sem, (h, mask), pair)

    def backward(block, h, first=False):
        for q in range(n_rep):
            term = jnp.dot(
                grads[block, h],
                dense[block, h * half:(h + 1) * half, q * rows:(q + 1) * rows],
                preferred_element_type=f32,
            )
            sums[q] = term if first else sums[q] + term

    def other(mask):
        return flip(z, mask) * cores + 1 - core

    share = feat // n_rep

    def w_rows(place):
        return pl.ds(pl.multiple_of(place * share, share), share)

    for h in range(halves):
        own_layer(h)
        send_own(h)
        piece = slice(h * half, (h + 1) * half)
        term = jnp.dot(agg_ref[piece, :].T, slope_ref[piece, :], preferred_element_type=f32)
        w_part[...] = term if h == 0 else w_part[...] + term
        backward(blk, h, h == 0)
    w_rep = [
        send(w_part.at[w_rows(flip(rep, m))], w_in.at[m], w_rep_sem, (m,), (flip(rep, m), blk))
        for m in range(1, n_rep)
    ]
    for h in range(halves):
        grad_pair[h, 0].wait_recv()
        backward(other(0), h)

    arrivals = [(h, mask) for h in range(halves) for mask in (skip, near, far)]
    for at, (h, mask) in enumerate(arrivals):
        take(h, mask)
        backward(line(mask), h)
        if at == 1:
            for copy in w_rep:
                copy.wait_recv()
            w_sum = w_part[w_rows(rep), :]
            for m in range(1, n_rep):
                w_sum = w_sum + w_in[m]
            w_pair_out[...] = w_sum
            w_pair = send(w_pair_out, w_pair_in, w_pair_sem, (0,), pair)
        grad_pair[h, mask].wait_recv()
        if at + 1 < len(arrivals):
            backward(other(mask), h)

    h, mask = arrivals[-1]
    last = other(mask)

    def finished(block):
        at = pl.ds(pl.multiple_of(block * rows, rows), rows)
        return sums[block] + jnp.dot(
            grads[last, h], dense[last, h * half:(h + 1) * half, at], preferred_element_type=f32
        )

    col_copies = {}
    for mask in reversed(range(1, n_rep)):
        target = flip(rep, mask)
        col_out[mask] = finished(target).astype(bf16)
        col_copies[mask] = send(
            col_out.at[mask], col_in.at[mask], col_sem, (mask,), (target, blk)
        )

    w_pair.wait_recv()
    w_line_out[...] = w_pair_out[...] + w_pair_in[...]
    w_line = [
        send(w_line_out, w_line_in.at[m], w_line_sem, (m,), line_device(m))
        for m in range(1, n_z)
    ]
    own_grads = jnp.concatenate([grads[blk, h] for h in range(halves)], axis=1)
    own_cols = finished(rep) + scale_ref[...] * own_grads.astype(f32)

    for copy in w_line:
        copy.wait_recv()
    w_all = w_line_out[...]
    for m in range(1, n_z):
        w_all = w_all + w_line_in[m]
    wgrad_ref[...] = w_all * inv_root

    for mask in range(1, n_rep):
        col_copies[mask].wait_recv()
        own_cols = own_cols + col_in[mask].astype(f32)
    fgrad_ref[...] = own_cols.T.astype(bf16)
    for copy, only in pending:
        if only is None:
            copy.wait_send()
        else:
            pl.when(only)(copy.wait_send)


def fused_layer(
    features, weight, cotangent, self_weight, block_rows, block_cols, block_counts, block_values
):
    n_rep = lax.axis_size("rep")
    n_blk = lax.axis_size("blk")
    n_z = n_blk // cores
    _, rows, feat = features.shape
    hidden = weight.shape[1]
    cap, side = block_values.shape[2:4]
    row_tiles = n_blk * rows // side
    col_tiles = n_rep * rows // side
    share = feat // n_rep
    f32, bf16 = jnp.float32, jnp.bfloat16

    map_lanes = 128
    map_rows = row_tiles * col_tiles // map_lanes
    vmem = pl.BlockSpec(memory_space=pltpu.VMEM)
    hbm = pl.BlockSpec(memory_space=pltpu.HBM)
    smem = pl.BlockSpec(memory_space=pltpu.SMEM)
    half = rows // halves
    dma = pltpu.SemaphoreType.DMA
    nodes = n_blk * n_rep * rows
    macs = nodes * n_rep * rows * feat // n_rep * 2
    activated, feature_grad, weight_grad = pl.pallas_call(
        functools.partial(layer_kernel, n_rep, n_blk, 1.0 / math.sqrt(nodes)),
        out_shape=(
            pltpu.VMEM((rows, hidden), bf16),
            pltpu.VMEM((rows, feat), bf16),
            pltpu.VMEM((share, hidden), f32),
        ),
        in_specs=[
            smem, smem, smem, hbm, hbm, hbm, vmem, hbm,
        ],
        out_specs=(vmem, vmem, vmem),
        scratch_shapes=[
            pltpu.VMEM((map_rows, map_lanes), jnp.int32),
            pltpu.SMEM((map_rows, map_lanes), jnp.int32),
            pltpu.VMEM((cap + 1, side, side), bf16),
            pltpu.VMEM((n_blk, rows, n_rep * rows), bf16),
            pltpu.VMEM((n_rep, rows, feat), bf16),
            pltpu.VMEM((feat, hidden), bf16),
            pltpu.VMEM((rows, hidden), bf16),
            pltpu.VMEM((halves, n_z, half, feat), bf16),
            pltpu.VMEM((halves, n_z, half, feat), bf16),
            pltpu.VMEM((halves, n_z, half, feat), bf16),
            pltpu.VMEM((halves, n_z, half, feat), bf16),
            pltpu.VMEM((halves, half, feat), bf16),
            pltpu.VMEM((halves, half, feat), f32),
            pltpu.VMEM((rows, feat), bf16),
            pltpu.VMEM((rows, hidden), bf16),
            pltpu.VMEM((n_blk, halves, feat, half), bf16),
            pltpu.VMEM((n_rep, feat, rows), f32),
            pltpu.VMEM((n_rep, feat, rows), bf16),
            pltpu.VMEM((n_rep, feat, rows), bf16),
            pltpu.VMEM((feat, hidden), f32),
            pltpu.VMEM((n_rep, share, hidden), f32),
            pltpu.VMEM((share, hidden), f32),
            pltpu.VMEM((share, hidden), f32),
            pltpu.VMEM((share, hidden), f32),
            pltpu.VMEM((n_z, share, hidden), f32),
            dma((load_parts + 4,)),
            dma((2, n_rep)),
            dma((2, halves, n_z)),
            dma((2, halves, n_z)),
            dma((2, halves, n_z)),
            dma((2, halves, n_z)),
            dma((2, n_rep)),
            dma((2, n_rep)),
            dma((2, 1)),
            dma((2, n_z)),
        ],
        compiler_params=pltpu.CompilerParams(
            collective_id=0, has_side_effects=True, vmem_limit_bytes=vmem_bytes
        ),
        cost_estimate=pl.CostEstimate(
            flops=2 * macs, bytes_accessed=cap * side * side * 2, transcendentals=rows * hidden
        ),
    )(
        block_rows[0], block_cols[0], block_counts,
        features[0], weight, cotangent[0], self_weight, block_values[0, 0],
    )
    return (activated[None], feature_grad[None], weight_grad)


def streamed_layer(
    features, weight, cotangent, self_weight, block_rows, block_cols, block_counts, block_values
):
    rows_dev = features.shape[1]
    feat_width = features.shape[2]
    tile_side = block_values.shape[-1]
    blk_count = lax.axis_size("blk")
    rep_count = lax.axis_size("rep")
    tile_values = block_values[0, 0]
    row_index = block_rows[0, 0]
    col_index = block_cols[0, 0]
    live_count = block_counts[0, 0]
    row_tiles = blk_count * rows_dev // tile_side
    col_tiles = rep_count * rows_dev // tile_side
    panel = lax.all_gather(features, "rep", axis=1, tiled=True)
    panel_tiles = panel.reshape(col_tiles, tile_side, feat_width)
    own_scale = self_weight[0][:, None]
    forward_terms = tile_products(
        tile_values, row_index, col_index, live_count, panel_tiles, row_tiles, False
    )
    forward_terms = forward_terms.reshape(blk_count, rows_dev, feat_width)
    summed_rows = lax.psum_scatter(
        forward_terms.astype(jnp.bfloat16), "blk", scatter_dimension=0, tiled=True
    ).astype(jnp.float32)[0]
    aggregated = (summed_rows + own_scale * features[0].astype(jnp.float32)).astype(jnp.bfloat16)
    pre_act = jnp.dot(aggregated, weight, preferred_element_type=jnp.float32)
    activated = jax.nn.silu(pre_act).astype(jnp.bfloat16)
    slope = (cotangent[0].astype(jnp.float32) * silu_slope(pre_act)).astype(jnp.bfloat16)
    node_total = blk_count * rep_count * rows_dev
    weight_part = jnp.einsum(
        "nf,nh->fh", aggregated, slope, preferred_element_type=jnp.float32
    ) / math.sqrt(node_total)
    row_grad = lax.dot_general(
        slope, weight, (((1,), (1,)), ((), ())), preferred_element_type=jnp.float32
    ).astype(jnp.bfloat16)
    all_grads = lax.all_gather(row_grad[None], "blk", axis=0, tiled=True)
    grad_tiles = all_grads.reshape(row_tiles, tile_side, feat_width)
    backward_terms = tile_products(
        tile_values, row_index, col_index, live_count, grad_tiles, col_tiles, True
    )
    backward_terms = backward_terms.reshape(1, rep_count * rows_dev, feat_width)
    own_grad = own_scale * row_grad.astype(jnp.float32)
    column_part = lax.psum_scatter(
        backward_terms.astype(jnp.bfloat16), "rep", scatter_dimension=1, tiled=True
    ).astype(jnp.float32)
    weight_full = lax.psum(weight_part, ("rep", "blk"))
    share_rows = weight_full.shape[0] // rep_count
    weight_grad = lax.dynamic_slice_in_dim(
        weight_full, lax.axis_index("rep") * share_rows, share_rows, 0
    )
    feature_grad = (column_part[0] + own_grad).astype(jnp.bfloat16)
    return (activated[None], feature_grad[None], weight_grad)


def on_device(*arrays):
    n_rep = lax.axis_size("rep")
    n_blk = lax.axis_size("blk")
    rows = arrays[0].shape[1]
    n_z = n_blk // cores
    fits = n_z == 4 and n_blk % cores == 0 and n_rep & (n_rep - 1) == 0
    side = arrays[-1].shape[-1]
    fits = fits and 128 % (n_rep * rows // side) == 0
    dense_bytes = 2 * n_blk * rows * n_rep * rows
    if fits and dense_bytes <= dense_limit:
        return fused_layer(*arrays)
    return streamed_layer(*arrays)


def solution(mesh):
    placed = (
        P("blk", "rep", None),
        P(),
        P("blk", "rep", None),
        P("blk", "rep"),
        P("rep", "blk", None),
        P("rep", "blk", None),
        P("rep", "blk"),
        P("rep", "blk", None, None, None),
    )
    return jax.shard_map(
        on_device,
        mesh=mesh,
        in_specs=placed,
        out_specs=(P("blk", "rep", None), P("blk", "rep", None), P("rep", None)),
        check_vma=False,
    )
```
